32 devices in a mesh: px: 4 (over x, core), py: 8 (over z, y).
Axes of the slice: x: 2, y: 2, z: 4, core: 2. Of those that a mesh axis runs over, the one named last changes fastest.
Arguments:
- adjoint: float32 [8, 8, 8, 1024], P('px', 'py'), may hold values from -6 to 6
- zone_ids: int32 [8, 8, 2], P('px', 'py'), may hold values from 0 to 7
- resist: float32 [8, 8, 2], P('px', 'py'), may hold values from 0.3 to 3
- tile_map: int32 [8, 8, 2], P('px', 'py'), may hold values from 0 to 63, as said below
- materials: float32 [3, 8, 14], replicated, may hold values from 0.2 to 1.5
Outputs:
- applied: float32 [3, 8, 8, 8, 1024], P(None, 'px', 'py')
- tile_grad: float32 [3, 64], P(None, ('px', 'py'))
The draws below stay inside these ranges and needn't reach their ends.
Inputs may be any that keep to these rules, and one draw needn't show every extreme that they name: `tile_map`: each design tile is a patch of 1 by 1 element columns through the whole thickness; in each row of patches the borders along the first direction may be shifted by one element, and a patch that crosses the panel's first-direction edge continues at the far edge. Tile numbers are in no spatial order, and every tile number occurs.
All inputs are finite; a program needn't handle non-finite values.
Results may differ from the reference program's by a relative error of at most 0.0001.
Values sent between devices are 32-bit elements; how exact they have to be, the bound alone decides.
A program may use at most 64 MiB of HBM per device.

```python
import math
import jax
import jax.numpy as jnp
import numpy as np
from jax import lax

NP = 8
FREQS = 3
ZONES = 8
COEFFS = 14
EZ = 2
TILE_DEV = 2
EX = 2
EY = 1
EXG = 8
EYG = 8
NODES = 1024
TILES = 64


def draw_tile_map(key, part):
    key = jax.random.fold_in(key, 11)
    shift_key, order_key = jax.random.split(key)
    patch_x = EX // TILE_DEV
    patch_rows = EYG // EY
    shifts = jax.random.randint(shift_key, (patch_rows,), 0, 2).astype(jnp.int32)
    first = jnp.arange(EXG, dtype=jnp.int32)
    second = jnp.arange(EYG, dtype=jnp.int32)
    coarse_second = second // EY
    coarse_first = (first[:, None] + shifts[coarse_second][None, :]) % EXG // patch_x
    base = coarse_first * patch_rows + coarse_second[None, :]
    order = jax.random.permutation(order_key, TILES).astype(jnp.int32)
    tiles = order[base]
    return jnp.broadcast_to(tiles[:, :, None], (EXG, EYG, EZ)).astype(jnp.int32)


def place_ends(values, own_key, smallest, top_value):
    index_at = [jax.random.randint(jax.random.fold_in(own_key, axis), (), 0, length) for axis, length in enumerate(values.shape)]
    longest = values.shape.index(max(values.shape))
    neighbour = index_at[:longest] + [(index_at[longest] + 1) % values.shape[longest]] + index_at[longest + 1:]
    return values.at[tuple(index_at)].set(smallest).at[tuple(neighbour)].set(top_value)


def steps_of(key, shape, shards, smallest, top_value):
    def one(axis_at, parts):
        steps = jax.random.uniform(jax.random.fold_in(jax.random.fold_in(key, 6), axis_at), (parts,), jnp.float32, smallest / len(shards), top_value / len(shards))
        return jnp.repeat(jnp.exp(steps), shape[axis_at] // parts).reshape((-1,) + (1,) * (len(shape) - axis_at - 1))

    level = one(*shards[0])
    for cut in shards[1:]:
        level = level * one(*cut)
    return level


def bell_draw(key, shape, spread, bound, pieces=(), kind=jnp.bfloat16):
    entries = spread * jax.random.normal(key, shape, jnp.float32)
    if pieces:
        entries = entries * steps_of(key, shape, pieces, -0.22, 0.18)
    return jnp.clip(entries, -bound, bound).astype(kind)


def setup_inputs(seed: int = 0) -> dict:
    key_of = jax.random.split(jax.random.key(seed), 6)
    adjoint = bell_draw(key_of[0], (EXG, EYG, 8, NODES), 1.0, 6.0, ((0, 4), (1, 8)), jnp.float32)
    zone_ids = place_ends(jax.random.randint(key_of[1], (EXG, EYG, EZ), 0, ZONES), jax.random.fold_in(key_of[1], 1), 0, ZONES - 1).astype(jnp.int32)
    resist = jnp.clip(jnp.exp(math.log(3.0) - 2.3025851 * jax.random.uniform(key_of[2], (EXG, EYG, EZ), jnp.float32) ** steps_of(key_of[2], (EXG, EYG, EZ), ((0, 4), (1, 8)), -0.2, 0.2)), 0.3, 3.0)
    tile_map = draw_tile_map(jax.random.fold_in(key_of[5], 71), 0)
    materials = jnp.clip(jax.random.uniform(key_of[4], (FREQS, ZONES, COEFFS), jnp.float32, 0.2, 1.5), 0.2, 1.5)
    return dict(adjoint=adjoint, zone_ids=zone_ids, resist=resist, tile_map=tile_map, materials=materials)


HIGHEST = lax.Precision.HIGHEST
GRAD_SCALE = 1e-3


def legendre_values(points, point_count):
    values = np.zeros((points.shape[0], point_count))
    values[:, 0] = 1.0
    values[:, 1] = points
    for degree in range(2, point_count):
        values[:, degree] = ((2 * degree - 1) * points * values[:, degree - 1] - (degree - 1) * values[:, degree - 2]) / degree
    return values


def lobatto(point_count):
    degree_top = point_count - 1
    points = np.cos(np.pi * np.arange(point_count) / degree_top)
    for newton_step in range(40):
        values = legendre_values(points, point_count)
        points = points - (points * values[:, degree_top] - values[:, degree_top - 1]) / (point_count * values[:, degree_top])
    points = points[::-1]
    top_values = legendre_values(points, point_count)[:, degree_top]
    weights = 2.0 / (degree_top * point_count * top_values ** 2)
    differ = np.zeros((point_count, point_count))
    for row_index in range(point_count):
        for column_index in range(point_count):
            if row_index != column_index:
                differ[row_index, column_index] = top_values[row_index] / (top_values[column_index] * (points[row_index] - points[column_index]))
    differ[0, 0] = -degree_top * point_count / 4.0
    differ[degree_top, degree_top] = degree_top * point_count / 4.0
    return weights, differ


def complex_times(left, right):
    return (left[0] * right[0] - left[1] * right[1], left[0] * right[1] + left[1] * right[0])


def complex_plus(left, right):
    return (left[0] + right[0], left[1] + right[1])


def channel_pair(source, channel):
    return (source[:, :, channel], source[:, :, channel + 4])


def coefficients(rows_table, resist):
    def conjugate(column):
        return (rows_table[..., column, None], -rows_table[..., column + 1, None])

    density = rows_table[..., 10]
    gain = rows_table[..., 11]
    damping = resist * gain
    modulus = density * density + damping * damping
    numerator = (rows_table[..., 8], rows_table[..., 9])
    mobility = complex_times(numerator, (density / modulus, damping / modulus))
    squared = modulus * modulus
    slope = complex_times(numerator, (-2.0 * density * damping * gain / squared, (density * density - damping * damping) * gain / squared))
    coeffs = (conjugate(0), conjugate(2), conjugate(4), conjugate(6), (mobility[0][..., None], -mobility[1][..., None]), conjugate(12))
    return coeffs, (slope[0], -slope[1])


def element_terms(gradients, values, coeffs, weight_cube):
    lame_first, shear, inertia, coupling, mobility, storage = coeffs
    displacement = [[channel_pair(gradients[direction], component) for direction in range(3)] for component in range(3)]
    divergence = complex_plus(complex_plus(displacement[0][0], displacement[1][1]), displacement[2][2])
    lame_term = complex_times(lame_first, divergence)
    fluxes = []
    for direction in range(3):
        real_parts = []
        imag_parts = []
        for component in range(3):
            symmetric = complex_plus(displacement[component][direction], displacement[direction][component])
            stress = complex_times(shear, symmetric)
            if component == direction:
                stress = complex_plus(stress, lame_term)
            real_parts.append(weight_cube * stress[0])
            imag_parts.append(weight_cube * stress[1])
        fluid = complex_times(mobility, channel_pair(gradients[direction], 3))
        drag = complex_times(coupling, channel_pair(values, direction))
        real_parts.append(weight_cube * (fluid[0] - drag[0]))
        imag_parts.append(weight_cube * (fluid[1] - drag[1]))
        fluxes.append(jnp.stack(real_parts + imag_parts, axis=2))
    real_parts = []
    imag_parts = []
    for component in range(3):
        inertial = complex_plus(complex_times(inertia, channel_pair(values, component)), complex_times(coupling, channel_pair(gradients[component], 3)))
        real_parts.append(-weight_cube * inertial[0])
        imag_parts.append(-weight_cube * inertial[1])
    compress = complex_times(storage, channel_pair(values, 3))
    real_parts.append(-weight_cube * compress[0])
    imag_parts.append(-weight_cube * compress[1])
    return fluxes, jnp.stack(real_parts + imag_parts, axis=2)


def element_energy(gradients, weight_cube):
    real_sum = jnp.zeros_like(gradients[0][:, :, 0])
    imag_sum = jnp.zeros_like(gradients[0][:, :, 0])
    for direction in range(3):
        real_part, imag_part = channel_pair(gradients[direction], 3)
        real_sum = real_sum + real_part * real_part - imag_part * imag_part
        imag_sum = imag_sum + 2.0 * real_part * imag_part
    return (jnp.sum(weight_cube * real_sum, axis=-1), jnp.sum(weight_cube * imag_sum, axis=-1))


def pair_sum(lower, upper, axis):
    size_along = upper.shape[axis]
    shared = lax.slice_in_dim(upper, 0, size_along - 1, axis=axis) + lax.slice_in_dim(lower, 1, size_along, axis=axis)
    new_upper = jnp.concatenate([shared, lax.slice_in_dim(upper, size_along - 1, size_along, axis=axis)], axis)
    new_lower = jnp.concatenate([lax.slice_in_dim(lower, 0, 1, axis=axis), shared], axis)
    return new_lower, new_upper


def assemble_local(nodal):
    batch, span_x, span_y, channels, length = nodal.shape
    layers = length // 512
    grid_view = nodal.reshape(batch, span_x, span_y, channels, length // 8, 8)
    lower, upper = pair_sum(grid_view[..., 0], grid_view[..., 7], 1)
    grid_view = grid_view.at[..., 0].set(lower).at[..., 7].set(upper)
    grid_view = grid_view.reshape(batch, span_x, span_y, channels, length // 64, 8, 8)
    lower, upper = pair_sum(grid_view[..., 0, :], grid_view[..., 7, :], 2)
    grid_view = grid_view.at[..., 0, :].set(lower).at[..., 7, :].set(upper)
    grid_view = grid_view.reshape(batch, span_x, span_y, channels, layers, 8, 64)
    lower, upper = pair_sum(grid_view[..., 0, :], grid_view[..., 7, :], 4)
    grid_view = grid_view.at[..., 0, :].set(lower).at[..., 7, :].set(upper)
    return grid_view.reshape(nodal.shape)


def reference(adjoint, zone_ids, resist, tile_map, materials):
    weights, differ = lobatto(NP)
    weight_cube = jnp.asarray((weights[:, None, None] * weights[None, :, None] * weights[None, None, :]).reshape(512), jnp.float32)
    derivative = jnp.asarray(differ, jnp.float32)
    span_x, span_y, channels, length = adjoint.shape
    layers = length // 512

    def derive(values):
        cube = values.reshape(values.shape[:-1] + (8, 8, 8))
        along_i = jnp.einsum('il,abczkjl->abczkji', derivative, cube, precision=HIGHEST)
        along_j = jnp.einsum('jl,abczklm->abczkjm', derivative, cube, precision=HIGHEST)
        along_k = jnp.einsum('kl,abczljm->abczkjm', derivative, cube, precision=HIGHEST)
        return [item.reshape(values.shape) for item in (along_i, along_j, along_k)]

    def derive_back(fluxes):
        cubes = [item.reshape(item.shape[:-1] + (8, 8, 8)) for item in fluxes]
        total = jnp.einsum('li,abczkjl->abczkji', derivative, cubes[0], precision=HIGHEST)
        total = total + jnp.einsum('lj,abczklm->abczkjm', derivative, cubes[1], precision=HIGHEST)
        total = total + jnp.einsum('lk,abczljm->abczkjm', derivative, cubes[2], precision=HIGHEST)
        return total.reshape(fluxes[0].shape)

    def row_apply(packed):
        row_values, row_table, row_resist = packed
        values = row_values.reshape(1, span_y, channels, layers, 512)
        gradients = derive(values)
        coeffs, slope = coefficients(row_table[None], row_resist[None])
        fluxes, local_term = element_terms(gradients, values, coeffs, weight_cube)
        return (derive_back(fluxes) + local_term).reshape(span_y, channels, length)

    def row_energy(row_values):
        values = row_values.reshape(1, span_y, channels, layers, 512)
        energy = element_energy(derive(values), weight_cube)
        return (energy[0][0], energy[1][0])

    outputs = []
    for frequency in range(FREQS):
        row_table = materials[frequency][zone_ids]
        element_result = lax.map(row_apply, (adjoint, row_table, resist))
        outputs.append(assemble_local(element_result[None])[0])
    applied = jnp.stack(outputs, axis=0)

    energy_real, energy_imag = lax.map(row_energy, adjoint)
    tile_grads = []
    for frequency in range(FREQS):
        coeffs, slope = coefficients(materials[frequency][zone_ids], resist)
        element_grad = GRAD_SCALE * complex_times(slope, (energy_real, energy_imag))[0]
        tile_grads.append(jax.ops.segment_sum(element_grad.reshape(-1), tile_map.reshape(-1), num_segments=TILES))
    return applied, jnp.stack(tile_grads, axis=0)
```

```python
import functools

import jax
import jax.numpy as jnp
import ml_dtypes
import numpy as np
from jax import lax
from jax.experimental import pallas as pl
from jax.experimental.pallas import tpu as pltpu
from jax.sharding import PartitionSpec as P

NP = 8
FREQS = 3
TILE_DEV = 2
CHANNELS = 8
GRAD_SCALE = 0.001
MESH = pl.DeviceIdType.MESH


def legendre_values(points, point_count):
    values = np.zeros((points.shape[0], point_count))
    values[:, 0] = 1.0
    values[:, 1] = points
    for degree in range(2, point_count):
        values[:, degree] = (
            (2 * degree - 1) * points * values[:, degree - 1] - (degree - 1) * values[:, degree - 2]
        ) / degree
    return values


def lobatto(point_count):
    degree_top = point_count - 1
    points = np.cos(np.pi * np.arange(point_count) / degree_top)
    for newton_step in range(40):
        values = legendre_values(points, point_count)
        points = points - (points * values[:, degree_top] - values[:, degree_top - 1]) / (
            point_count * values[:, degree_top]
        )
    points = points[::-1]
    top_values = legendre_values(points, point_count)[:, degree_top]
    weights = 2.0 / (degree_top * point_count * top_values**2)
    differ = np.zeros((point_count, point_count))
    for row_index in range(point_count):
        for column_index in range(point_count):
            if row_index != column_index:
                differ[row_index, column_index] = top_values[row_index] / (
                    top_values[column_index] * (points[row_index] - points[column_index])
                )
    differ[0, 0] = -degree_top * point_count / 4.0
    differ[degree_top, degree_top] = degree_top * point_count / 4.0
    return (weights, differ)


def split_np(matrix):
    matrix = matrix.astype(np.float32)
    hi = matrix.astype(ml_dtypes.bfloat16)
    lo = (matrix - hi.astype(np.float32)).astype(ml_dtypes.bfloat16)
    return hi, lo


def tables():
    weights, differ = lobatto(NP)
    order = np.array([0, 2, 4, 6, 1, 3, 5, 7])
    weight = weights[order][:, None] * np.tile(np.kron(weights, weights), 2)[None, :]
    along_i = np.kron(np.eye(16), differ)
    along_j = np.kron(np.eye(2), np.kron(differ, np.eye(8)))
    along_k = np.kron(np.eye(16), differ[order][:, order])
    fwd_hi, fwd_lo = split_np(np.concatenate([along_i.T, along_j.T], axis=1))
    back_hi, back_lo = split_np(np.concatenate([along_i, along_j], axis=0))
    k_hi, k_lo = split_np(along_k)
    kt_hi, kt_lo = split_np(along_k.T)
    return (
        np.concatenate([fwd_hi, fwd_lo, fwd_hi], axis=0),
        np.concatenate([k_hi, k_hi, k_lo], axis=1),
        np.concatenate([back_hi, back_lo, back_hi], axis=0),
        np.concatenate([kt_hi, kt_hi, kt_lo], axis=1),
        np.tile(weight, (2, 1)).astype(np.float32),
    )


def split(values):
    hi = values.astype(jnp.bfloat16)
    lo = (values - hi.astype(jnp.float32)).astype(jnp.bfloat16)
    return hi, lo


def conj_times(c, x):
    return (c[0] * x[0] + c[1] * x[1], c[0] * x[1] - c[1] * x[0])


def plus(left, right):
    return (left[0] + right[0], left[1] + right[1])


def minus(left, right):
    return (left[0] - right[0], left[1] - right[1])


def body(
    npx,
    npy,
    x_ref,
    zone_ref,
    resist_ref,
    tile_ref,
    mat_ref,
    fwd_ref,
    fwdk_ref,
    back_ref,
    backk_ref,
    weight_ref,
    out_ref,
    grad_ref,
    held,
    sxb,
    syb,
    rx,
    ry,
    rc,
    g1,
    g2,
    x_send,
    x_recv,
    y_send,
    y_recv,
    c_send,
    c_recv,
    g1_send,
    g1_recv,
    g2_send,
    g2_recv,
):
    f32 = jnp.float32
    px, py = lax.axis_index("px"), lax.axis_index("py")
    to_x = (px - 1, px + 1)
    to_y = (py - 1, py + 1)
    has_x = (px > 0, px < npx - 1)
    has_y = (py > 0, py < npy - 1)
    corners = [(i, j) for i in range(2) for j in range(2)]

    def has_corner(i, j):
        return jnp.logical_and(has_x[i], has_y[j])

    def peer_px(d):
        return (lax.rem(px + d, npx), py)

    def peer_py(d):
        return (px, lax.rem(py + d, npy))

    def over(count, step):
        if count <= 8:
            for d in range(1, count):
                step(d)
        else:
            lax.fori_loop(1, count, lambda d, carry: (step(d), carry)[1], 0)

    barrier = pltpu.get_barrier_semaphore()

    def greet(device):
        pl.semaphore_signal(barrier, inc=1, device_id=device, device_id_type=MESH)

    over(npx, lambda d: greet(peer_px(d)))
    over(npy, lambda d: greet(peer_py(d)))
    for i, j in corners:

        @pl.when(has_corner(i, j))
        def _(i=i, j=j):
            greet((to_x[i], to_y[j]))

    x_sides = jnp.where(has_x[0], 1, 0) + jnp.where(has_x[1], 1, 0)
    y_sides = jnp.where(has_y[0], 1, 0) + jnp.where(has_y[1], 1, 0)

    row = lax.broadcasted_iota(jnp.int32, (8, 128), 0)
    lane = lax.broadcasted_iota(jnp.int32, (8, 128), 1)
    low = lane < 64
    keep = (row < 4) == low
    at_i = (lane % 8 == 0, lane % 8 == 7)
    at_j = ((lane // 8) % 8 == 0, (lane // 8) % 8 == 7)
    slot_i = [lane % 8 == m for m in range(8)]
    slot_j = [(lane // 8) % 8 == m for m in range(8)]
    seam_low = jnp.logical_and(row == 3, lane >= 64)
    seam_high = jnp.logical_and(row == 4, low)

    def lane_roll(block, shift):
        shift = shift % 128
        return block if shift == 0 else pltpu.roll(block, shift, 1)

    def swap(block):
        return jnp.where(keep, block, pltpu.roll(lane_roll(block, 64), 4, 0))

    for i in range(2):

        @pl.when(jnp.logical_not(has_x[i]))
        def _(i=i):
            rx[i] = jnp.zeros((FREQS, 8, 128), f32)

        @pl.when(jnp.logical_not(has_y[i]))
        def _(i=i):
            ry[i] = jnp.zeros((2, FREQS, 8, 128), f32)

    for i, j in corners:

        @pl.when(jnp.logical_not(has_corner(i, j)))
        def _(i=i, j=j):
            rc[2 * i + j] = jnp.zeros((FREQS, 8, 128), f32)

    blocks = []
    for m in range(CHANNELS):
        for a in range(2):
            blocks.append(swap(x_ref[pl.ds(64 * a + m, 8, stride=8), :]))
    nodal = jnp.concatenate(blocks, axis=0)
    hi, lo = split(nodal)
    first_two = jnp.dot(
        jnp.concatenate([hi, hi, lo], axis=1), fwd_ref[...], preferred_element_type=f32
    )
    third = jnp.dot(
        fwdk_ref[...], jnp.concatenate([hi, lo, hi], axis=0), preferred_element_type=f32
    )
    raw = (first_two[:, :128], first_two[:, 128:], third)
    weight = weight_ref[...]

    def channel(source, m):
        return source[16 * m : 16 * m + 16]

    def pair(source, m):
        return (weight * channel(source, m), weight * channel(source, m + 4))

    u = [pair(nodal, m) for m in range(4)]
    g = [[pair(raw[d], m) for m in range(4)] for d in range(3)]

    zones = [[zone_ref[a, 0, c] for c in range(2)] for a in range(2)]

    def spread(get):
        return jnp.concatenate(
            [jnp.where(low, get(a, 0), get(a, 1)) for a in range(2)], axis=0
        )

    resist = spread(lambda a, c: resist_ref[a, 0, c])
    coeffs = []
    slopes = []
    for f in range(FREQS):
        col = [spread(lambda a, c: mat_ref[f, zones[a][c], n]) for n in range(14)]
        density, gain = col[10], col[11]
        damping = resist * gain
        inverse = 1.0 / (density * density + damping * damping)
        real, imag = density * inverse, damping * inverse
        mobility = (col[8] * real - col[9] * imag, col[8] * imag + col[9] * real)
        square = gain * inverse * inverse
        real = -2.0 * density * damping * square
        imag = (density * density - damping * damping) * square
        slopes.append((col[8] * real - col[9] * imag, col[8] * imag + col[9] * real))
        coeffs.append(
            (
                (col[0], col[1]),
                (col[2], col[3]),
                (col[4], col[5]),
                (col[6], col[7]),
                mobility,
                (col[12], col[13]),
            )
        )

    energy_real = jnp.zeros((16, 128), f32)
    energy_imag = jnp.zeros((16, 128), f32)
    for d in range(3):
        real, imag = channel(raw[d], 3), channel(raw[d], 7)
        energy_real += g[d][3][0] * real - g[d][3][1] * imag
        energy_imag += g[d][3][0] * imag
    energy_imag = 2.0 * energy_imag
    width = g1.shape[2]
    wide = lax.broadcasted_iota(jnp.int32, (8, width), 1)
    wide_row = lax.broadcasted_iota(jnp.int32, (8, width), 0)
    message = jnp.zeros((8, width), f32)
    for f in range(FREQS):
        density = GRAD_SCALE * (slopes[f][0] * energy_real + slopes[f][1] * energy_imag)
        gathered = jnp.zeros((8, width), f32)
        for a in range(2):
            part = density[8 * a : 8 * a + 8]
            for c in range(2):
                mine = jnp.where(low, part, 0.0) if c == 0 else jnp.where(low, 0.0, part)
                mine = jnp.sum(mine, axis=1, keepdims=True)
                gathered += jnp.where(wide == tile_ref[a, 0, c], mine, 0.0)
        gathered = jnp.sum(gathered, axis=0, keepdims=True)
        message = jnp.where(wide_row == f, gathered, message)
    g1[0] = message

    pl.semaphore_wait(barrier, npx - 1 + npy - 1 + x_sides * y_sides)

    def copy_g1(d):
        return pltpu.make_async_remote_copy(
            src_ref=g1.at[0],
            dst_ref=g1.at[d],
            send_sem=g1_send.at[d],
            recv_sem=g1_recv.at[d],
            device_id=peer_px(d),
            device_id_type=MESH,
        )

    def copy_g2(d):
        return pltpu.make_async_remote_copy(
            src_ref=g2.at[0],
            dst_ref=g2.at[d],
            send_sem=g2_send.at[d],
            recv_sem=g2_recv.at[d],
            device_id=peer_py(d),
            device_id_type=MESH,
        )

    over(npx, lambda d: copy_g1(d).start())

    div = plus(plus(g[0][0], g[1][1]), g[2][2])
    sym = {}
    for m in range(3):
        for d in range(m, 3):
            sym[m, d] = plus(g[d][m], g[m][d])

    for f in range(FREQS):
        lame, shear, inertia, coupling, mobility, storage = coeffs[f]
        lame_term = conj_times(lame, div)
        stress = {}
        for (m, d), value in sym.items():
            item = conj_times(shear, value)
            if m == d:
                item = plus(item, lame_term)
            stress[m, d] = stress[d, m] = item
        flux = []
        for d in range(3):
            fluid = minus(conj_times(mobility, g[d][3]), conj_times(coupling, u[d]))
            items = [stress[m, d] for m in range(3)] + [fluid]
            flux.append(
                split(
                    jnp.concatenate([item[0] for item in items] + [item[1] for item in items], axis=0)
                )
            )
        items = [
            plus(conj_times(inertia, u[m]), conj_times(coupling, g[m][3])) for m in range(3)
        ] + [conj_times(storage, u[3])]
        local = jnp.concatenate([item[0] for item in items] + [item[1] for item in items], axis=0)
        (i_hi, i_lo), (j_hi, j_lo), (k_hi, k_lo) = flux
        total = jnp.dot(
            jnp.concatenate([i_hi, j_hi, i_hi, j_hi, i_lo, j_lo], axis=1),
            back_ref[...],
            preferred_element_type=f32,
        )
        total += jnp.dot(
            backk_ref[...], jnp.concatenate([k_hi, k_lo, k_hi], axis=0), preferred_element_type=f32
        )
        total -= local
        packed_x = [jnp.zeros((8, 128), f32)] * 2
        packed_y = [[jnp.zeros((8, 128), f32)] * 2 for _ in range(2)]
        for m in range(CHANNELS):
            both = []
            for a in range(2):
                block = swap(total[16 * m + 8 * a : 16 * m + 8 * a + 8])
                turned = lane_roll(block, 64)
                block = (
                    block
                    + jnp.where(seam_low, pltpu.roll(turned, 7, 0), 0.0)
                    + jnp.where(seam_high, pltpu.roll(turned, 1, 0), 0.0)
                )
                both.append(block)
            left, right = both
            both = [
                left + jnp.where(at_i[1], lane_roll(right, 7), 0.0),
                right + jnp.where(at_i[0], lane_roll(left, -7), 0.0),
            ]
            for s in range(2):
                packed_x[s] = jnp.where(slot_i[m], lane_roll(both[s], m - 7 * s), packed_x[s])
                for a in range(2):
                    packed_y[s][a] = jnp.where(
                        slot_j[m], lane_roll(both[a], 8 * (m - 7 * s)), packed_y[s][a]
                    )
            for a in range(2):
                held[f, 2 * m + a] = both[a]
        for s in range(2):
            sxb[s, f] = packed_x[s]
            for a in range(2):
                syb[s, a, f] = packed_y[s][a]

    def copy_x(s, there):
        return pltpu.make_async_remote_copy(
            src_ref=sxb.at[s],
            dst_ref=rx.at[there],
            send_sem=x_send.at[s],
            recv_sem=x_recv.at[there],
            device_id=(to_x[s], py),
            device_id_type=MESH,
        )

    def copy_y(s, there):
        return pltpu.make_async_remote_copy(
            src_ref=syb.at[s],
            dst_ref=ry.at[there],
            send_sem=y_send.at[s],
            recv_sem=y_recv.at[there],
            device_id=(px, to_y[s]),
            device_id_type=MESH,
        )

    def copy_c(i, j, there):
        return pltpu.make_async_remote_copy(
            src_ref=syb.at[j, i],
            dst_ref=rc.at[there],
            send_sem=c_send.at[2 * i + j],
            recv_sem=c_recv.at[there],
            device_id=(to_x[i], to_y[j]),
            device_id_type=MESH,
        )

    for s in range(2):

        @pl.when(has_y[s])
        def _(s=s):
            copy_y(s, 1 - s).start()

    for i, j in corners:

        @pl.when(has_corner(i, j))
        def _(i=i, j=j):
            copy_c(i, j, 3 - 2 * i - j).start()

    for s in range(2):

        @pl.when(has_x[s])
        def _(s=s):
            copy_x(s, 1 - s).start()

    over(npx, lambda d: copy_g1(d).wait())
    column = g1[0]
    for d in range(1, npx):
        column += g1[d]
    g2[0] = column
    over(npy, lambda d: copy_g2(d).start())

    for s in range(2):

        @pl.when(has_x[s])
        def _(s=s):
            copy_x(s, s).wait()

    for s in range(2):

        @pl.when(has_y[s])
        def _(s=s):
            copy_y(s, s).wait()

    for i, j in corners:

        @pl.when(has_corner(i, j))
        def _(i=i, j=j):
            copy_c(i, j, 2 * i + j).wait()

    for f in range(FREQS):
        from_x = [rx[s, f] for s in range(2)]
        from_y = []
        for s in range(2):
            side = []
            for a in range(2):
                corner = lane_roll(rc[2 * a + s, f], 7 * (2 * a - 1))
                side.append(ry[s, a, f] + jnp.where(at_i[a], corner, 0.0))
            from_y.append(side)
        for m in range(CHANNELS):
            for a in range(2):
                block = held[f, 2 * m + a]
                block += jnp.where(at_i[a], lane_roll(from_x[a], 7 * a - m), 0.0)
                for s in range(2):
                    block += jnp.where(
                        at_j[s], lane_roll(from_y[s][a], 8 * (7 * s - m)), 0.0
                    )
                out_ref[pl.ds(128 * f + 64 * a + m, 8, stride=8), :] = block

    over(npy, lambda d: copy_g2(d).wait())
    if npy <= 8:
        column = g2[0]
        for d in range(1, npy):
            column += g2[d]
    else:
        column = lax.fori_loop(1, npy, lambda d, carry: carry + g2[d], g2[0])
    first = TILE_DEV * (px * npy + py)
    pieces = [
        jnp.sum(jnp.where(wide == first + q, column, 0.0), axis=1, keepdims=True)
        for q in range(TILE_DEV)
    ]
    grad_ref[...] = jnp.concatenate(pieces, axis=1)[:FREQS]


def on_device(npx, npy, adjoint, zone_ids, resist, tile_map, materials):
    f32 = jnp.float32
    view = adjoint.reshape(2, 8, 8, 128).transpose(0, 2, 1, 3).reshape(128, 128)
    width = -(-TILE_DEV * npx * npy // 128) * 128
    vmem = pl.BlockSpec(memory_space=pltpu.VMEM)
    smem = pl.BlockSpec(memory_space=pltpu.SMEM)
    dma = pltpu.SemaphoreType.DMA
    out, grad = pl.pallas_call(
        functools.partial(body, npx, npy),
        out_shape=(
            jax.ShapeDtypeStruct((FREQS * 128, 128), f32),
            jax.ShapeDtypeStruct((FREQS, TILE_DEV), f32),
        ),
        in_specs=[vmem] + [smem] * 4 + [vmem] * 5,
        out_specs=(vmem, vmem),
        scratch_shapes=[
            pltpu.VMEM((FREQS, 16, 8, 128), f32),
            pltpu.VMEM((2, FREQS, 8, 128), f32),
            pltpu.VMEM((2, 2, FREQS, 8, 128), f32),
            pltpu.VMEM((2, FREQS, 8, 128), f32),
            pltpu.VMEM((2, 2, FREQS, 8, 128), f32),
            pltpu.VMEM((4, FREQS, 8, 128), f32),
            pltpu.VMEM((npx, 8, width), f32),
            pltpu.VMEM((npy, 8, width), f32),
            dma((2,)),
            dma((2,)),
            dma((2,)),
            dma((2,)),
            dma((4,)),
            dma((4,)),
            dma((npx,)),
            dma((npx,)),
            dma((npy,)),
            dma((npy,)),
        ],
        compiler_params=pltpu.CompilerParams(
            collective_id=0, has_side_effects=True, vmem_limit_bytes=32 * 1024 * 1024
        ),
    )(view, zone_ids, resist, tile_map, materials, *[jnp.asarray(item) for item in tables()])
    applied = out.reshape(FREQS, 2, 8, 8, 128).transpose(0, 1, 3, 2, 4)
    return (applied.reshape(FREQS, 2, 1, CHANNELS, 1024), grad)


def solution(mesh):
    in_specs = (
        P("px", "py", None, None),
        P("px", "py", None),
        P("px", "py", None),
        P("px", "py", None),
        P(),
    )
    out_specs = (P(None, "px", "py", None, None), P(None, ("px", "py")))
    return jax.shard_map(
        functools.partial(on_device, mesh.shape["px"], mesh.shape["py"]),
        mesh=mesh,
        in_specs=in_specs,
        out_specs=out_specs,
        check_vma=False,
    )
```

```python
import functools

import jax
import jax.numpy as jnp
import ml_dtypes
import numpy as np
from jax import lax
from jax.experimental import pallas as pl
from jax.experimental.pallas import tpu as pltpu
from jax.sharding import PartitionSpec as P

NP = 8
FREQS = 3
TILE_DEV = 2
CHANNELS = 8
GRAD_SCALE = 0.001
MESH = pl.DeviceIdType.MESH


def legendre_values(points, point_count):
    values = np.zeros((points.shape[0], point_count))
    values[:, 0] = 1.0
    values[:, 1] = points
    for degree in range(2, point_count):
        values[:, degree] = (
            (2 * degree - 1) * points * values[:, degree - 1] - (degree - 1) * values[:, degree - 2]
        ) / degree
    return values


def lobatto(point_count):
    degree_top = point_count - 1
    points = np.cos(np.pi * np.arange(point_count) / degree_top)
    for newton_step in range(40):
        values = legendre_values(points, point_count)
        points = points - (points * values[:, degree_top] - values[:, degree_top - 1]) / (
            point_count * values[:, degree_top]
        )
    points = points[::-1]
    top_values = legendre_values(points, point_count)[:, degree_top]
    weights = 2.0 / (degree_top * point_count * top_values**2)
    differ = np.zeros((point_count, point_count))
    for row_index in range(point_count):
        for column_index in range(point_count):
            if row_index != column_index:
                differ[row_index, column_index] = top_values[row_index] / (
                    top_values[column_index] * (points[row_index] - points[column_index])
                )
    differ[0, 0] = -degree_top * point_count / 4.0
    differ[degree_top, degree_top] = degree_top * point_count / 4.0
    return (weights, differ)


def split_np(matrix):
    matrix = matrix.astype(np.float32)
    hi = matrix.astype(ml_dtypes.bfloat16)
    lo = (matrix - hi.astype(np.float32)).astype(ml_dtypes.bfloat16)
    return hi, lo


def tables():
    weights, differ = lobatto(NP)
    order = np.array([0, 2, 4, 6, 1, 3, 5, 7])
    weight = weights[order][:, None] * np.tile(np.kron(weights, weights), 2)[None, :]
    along_i = np.kron(np.eye(16), differ)
    along_j = np.kron(np.eye(2), np.kron(differ, np.eye(8)))
    along_k = np.kron(np.eye(16), differ[order][:, order])
    fwd_hi, fwd_lo = split_np(np.concatenate([along_i.T, along_j.T], axis=1))
    back_hi, back_lo = split_np(np.concatenate([along_i, along_j], axis=0))
    k_hi, k_lo = split_np(along_k)
    kt_hi, kt_lo = split_np(along_k.T)
    forward = np.concatenate([fwd_hi, fwd_lo, fwd_hi], axis=0)
    return (
        np.concatenate([forward[:, :128], forward[:, 128:], k_hi, k_hi, k_lo], axis=0),
        np.concatenate([back_hi, back_lo, back_hi, kt_hi, kt_hi, kt_lo], axis=0),
        np.tile(weight, (2, 1)).astype(np.float32),
    )


def split(values):
    hi = values.astype(jnp.bfloat16)
    lo = (values - hi.astype(jnp.float32)).astype(jnp.bfloat16)
    return hi, lo


def conj_times(c, x):
    return (c[0] * x[0] + c[1] * x[1], c[0] * x[1] - c[1] * x[0])


def plus(left, right):
    return (left[0] + right[0], left[1] + right[1])


def minus(left, right):
    return (left[0] - right[0], left[1] - right[1])


def body(
    npx,
    npy,
    x_hbm,
    zone_hbm,
    resist_hbm,
    tile_hbm,
    mat_hbm,
    forward_hbm,
    backward_hbm,
    weight_hbm,
    out_ref,
    grad_ref,
    x_ref,
    zone_ref,
    resist_ref,
    tile_ref,
    mat_ref,
    forward_ref,
    backward_ref,
    weight_ref,
    load_sem,
    held,
    sxb,
    syb,
    rx,
    ry,
    rc,
    g1,
    g2,
    x_send,
    x_recv,
    y_send,
    y_recv,
    c_send,
    c_recv,
    g1_send,
    g1_recv,
    g2_send,
    g2_recv,
):
    f32 = jnp.float32
    loads = [
        pltpu.make_async_copy(source, target, load_sem.at[n])
        for n, (source, target) in enumerate(
            (
                (x_hbm, x_ref),
                (forward_hbm, forward_ref),
                (weight_hbm, weight_ref),
                (zone_hbm, zone_ref),
                (resist_hbm, resist_ref),
                (mat_hbm, mat_ref),
                (tile_hbm, tile_ref),
                (backward_hbm, backward_ref),
            )
        )
    ]
    for load in loads:
        load.start()
    px, py = lax.axis_index("px"), lax.axis_index("py")
    to_x = (px - 1, px + 1)
    to_y = (py - 1, py + 1)
    has_x = (px > 0, px < npx - 1)
    has_y = (py > 0, py < npy - 1)
    corners = [(i, j) for i in range(2) for j in range(2)]

    def has_corner(i, j):
        return jnp.logical_and(has_x[i], has_y[j])

    def peer_px(d):
        return (lax.rem(px + d, npx), py)

    def peer_py(d):
        return (px, lax.rem(py + d, npy))

    def over(count, step):
        if count <= 8:
            for d in range(1, count):
                step(d)
        else:
            lax.fori_loop(1, count, lambda d, carry: (step(d), carry)[1], 0)

    barrier = pltpu.get_barrier_semaphore()

    def greet(device):
        pl.semaphore_signal(barrier, inc=1, device_id=device, device_id_type=MESH)

    over(npx, lambda d: greet(peer_px(d)))
    over(npy, lambda d: greet(peer_py(d)))
    for i, j in corners:

        @pl.when(has_corner(i, j))
        def _(i=i, j=j):
            greet((to_x[i], to_y[j]))

    x_sides = jnp.where(has_x[0], 1, 0) + jnp.where(has_x[1], 1, 0)
    y_sides = jnp.where(has_y[0], 1, 0) + jnp.where(has_y[1], 1, 0)

    row = lax.broadcasted_iota(jnp.int32, (8, 128), 0)
    lane = lax.broadcasted_iota(jnp.int32, (8, 128), 1)
    low = lane < 64
    keep = (row < 4) == low
    at_i = (lane % 8 == 0, lane % 8 == 7)
    at_j = ((lane // 8) % 8 == 0, (lane // 8) % 8 == 7)
    slot_i = [lane % 8 == m for m in range(8)]
    slot_j = [(lane // 8) % 8 == m for m in range(8)]
    seam_low = jnp.logical_and(row == 3, lane >= 64)
    seam_high = jnp.logical_and(row == 4, low)

    def lane_roll(block, shift):
        shift = shift % 128
        return block if shift == 0 else pltpu.roll(block, shift, 1)

    def swap(block):
        return jnp.where(keep, block, pltpu.roll(lane_roll(block, 64), 4, 0))

    for i in range(2):

        @pl.when(jnp.logical_not(has_x[i]))
        def _(i=i):
            rx[i] = jnp.zeros((FREQS, 8, 128), f32)

        @pl.when(jnp.logical_not(has_y[i]))
        def _(i=i):
            ry[i] = jnp.zeros((2, FREQS, 8, 128), f32)

    for i, j in corners:

        @pl.when(jnp.logical_not(has_corner(i, j)))
        def _(i=i, j=j):
            rc[2 * i + j] = jnp.zeros((FREQS, 8, 128), f32)

    loads[0].wait()
    blocks = []
    for m in range(CHANNELS):
        for a in range(2):
            blocks.append(swap(x_ref[pl.ds(64 * a + m, 8, stride=8), :]))
    nodal = jnp.concatenate(blocks, axis=0)
    hi, lo = split(nodal)
    loads[1].wait()
    wide_nodal = jnp.concatenate([hi, hi, lo], axis=1)
    first = jnp.dot(wide_nodal, forward_ref[0:384, :], preferred_element_type=f32)
    second = jnp.dot(wide_nodal, forward_ref[384:768, :], preferred_element_type=f32)

    def left(ref, base, tall):
        k_parts = [ref[base + 128 * n : base + 128 * n + 128, :] for n in range(3)]
        return jnp.dot(jnp.concatenate(k_parts, axis=1), tall, preferred_element_type=f32)

    third = left(forward_ref, 768, jnp.concatenate([hi, lo, hi], axis=0))
    raw = (first, second, third)
    loads[2].wait()
    weight = weight_ref[...]

    def channel(source, m):
        return source[16 * m : 16 * m + 16]

    def pair(source, m):
        return (weight * channel(source, m), weight * channel(source, m + 4))

    u = [pair(nodal, m) for m in range(4)]
    g = [[pair(raw[d], m) for m in range(4)] for d in range(3)]

    for load in loads[3:7]:
        load.wait()
    zones = [[zone_ref[a, 0, c] for c in range(2)] for a in range(2)]

    def spread(get):
        return jnp.concatenate(
            [jnp.where(low, get(a, 0), get(a, 1)) for a in range(2)], axis=0
        )

    resist = spread(lambda a, c: resist_ref[a, 0, c])
    coeffs = []
    slopes = []
    for f in range(FREQS):
        col = [spread(lambda a, c: mat_ref[f, zones[a][c], n]) for n in range(14)]
        density, gain = col[10], col[11]
        damping = resist * gain
        inverse = 1.0 / (density * density + damping * damping)
        real, imag = density * inverse, damping * inverse
        mobility = (col[8] * real - col[9] * imag, col[8] * imag + col[9] * real)
        square = gain * inverse * inverse
        real = -2.0 * density * damping * square
        imag = (density * density - damping * damping) * square
        slopes.append((col[8] * real - col[9] * imag, col[8] * imag + col[9] * real))
        coeffs.append(
            (
                (col[0], col[1]),
                (col[2], col[3]),
                (col[4], col[5]),
                (col[6], col[7]),
                mobility,
                (col[12], col[13]),
            )
        )

    energy_real = jnp.zeros((16, 128), f32)
    energy_imag = jnp.zeros((16, 128), f32)
    for d in range(3):
        real, imag = channel(raw[d], 3), channel(raw[d], 7)
        energy_real += g[d][3][0] * real - g[d][3][1] * imag
        energy_imag += g[d][3][0] * imag
    energy_imag = 2.0 * energy_imag
    width = g1.shape[2]
    wide = lax.broadcasted_iota(jnp.int32, (8, width), 1)
    wide_row = lax.broadcasted_iota(jnp.int32, (8, width), 0)
    message = jnp.zeros((8, width), f32)
    for f in range(FREQS):
        density = GRAD_SCALE * (slopes[f][0] * energy_real + slopes[f][1] * energy_imag)
        gathered = jnp.zeros((8, width), f32)
        for a in range(2):
            part = density[8 * a : 8 * a + 8]
            for c in range(2):
                mine = jnp.where(low, part, 0.0) if c == 0 else jnp.where(low, 0.0, part)
                mine = jnp.sum(mine, axis=1, keepdims=True)
                gathered += jnp.where(wide == tile_ref[a, 0, c], mine, 0.0)
        gathered = jnp.sum(gathered, axis=0, keepdims=True)
        message = jnp.where(wide_row == f, gathered, message)
    g1[0] = message

    pl.semaphore_wait(barrier, npx - 1 + npy - 1 + x_sides * y_sides)

    def copy_g1(d):
        return pltpu.make_async_remote_copy(
            src_ref=g1.at[0],
            dst_ref=g1.at[d],
            send_sem=g1_send.at[d],
            recv_sem=g1_recv.at[d],
            device_id=peer_px(d),
            device_id_type=MESH,
        )

    def copy_g2(d):
        return pltpu.make_async_remote_copy(
            src_ref=g2.at[0],
            dst_ref=g2.at[d],
            send_sem=g2_send.at[d],
            recv_sem=g2_recv.at[d],
            device_id=peer_py(d),
            device_id_type=MESH,
        )

    over(npx, lambda d: copy_g1(d).start())

    div = plus(plus(g[0][0], g[1][1]), g[2][2])
    sym = {}
    for m in range(3):
        for d in range(m, 3):
            sym[m, d] = plus(g[d][m], g[m][d])

    loads[7].wait()
    for f in range(FREQS):
        lame, shear, inertia, coupling, mobility, storage = coeffs[f]
        lame_term = conj_times(lame, div)
        stress = {}
        for (m, d), value in sym.items():
            item = conj_times(shear, value)
            if m == d:
                item = plus(item, lame_term)
            stress[m, d] = stress[d, m] = item
        flux = []
        for d in range(3):
            fluid = minus(conj_times(mobility, g[d][3]), conj_times(coupling, u[d]))
            items = [stress[m, d] for m in range(3)] + [fluid]
            flux.append(
                split(
                    jnp.concatenate([item[0] for item in items] + [item[1] for item in items], axis=0)
                )
            )
        items = [
            plus(conj_times(inertia, u[m]), conj_times(coupling, g[m][3])) for m in range(3)
        ] + [conj_times(storage, u[3])]
        local = jnp.concatenate([item[0] for item in items] + [item[1] for item in items], axis=0)
        (i_hi, i_lo), (j_hi, j_lo), (k_hi, k_lo) = flux
        total = jnp.dot(
            jnp.concatenate([i_hi, j_hi, i_hi, j_hi, i_lo, j_lo], axis=1),
            backward_ref[0:768, :],
            preferred_element_type=f32,
        )
        total += left(backward_ref, 768, jnp.concatenate([k_hi, k_lo, k_hi], axis=0))
        total -= local
        packed_x = [jnp.zeros((8, 128), f32)] * 2
        packed_y = [[jnp.zeros((8, 128), f32)] * 2 for _ in range(2)]
        for m in range(CHANNELS):
            both = []
            for a in range(2):
                block = swap(total[16 * m + 8 * a : 16 * m + 8 * a + 8])
                turned = lane_roll(block, 64)
                block = (
                    block
                    + jnp.where(seam_low, pltpu.roll(turned, 7, 0), 0.0)
                    + jnp.where(seam_high, pltpu.roll(turned, 1, 0), 0.0)
                )
                both.append(block)
            lower, upper = both
            both = [
                lower + jnp.where(at_i[1], lane_roll(upper, 7), 0.0),
                upper + jnp.where(at_i[0], lane_roll(lower, -7), 0.0),
            ]
            for s in range(2):
                packed_x[s] = jnp.where(slot_i[m], lane_roll(both[s], m - 7 * s), packed_x[s])
                for a in range(2):
                    packed_y[s][a] = jnp.where(
                        slot_j[m], lane_roll(both[a], 8 * (m - 7 * s)), packed_y[s][a]
                    )
            for a in range(2):
                held[f, 2 * m + a] = both[a]
        for s in range(2):
            sxb[s, f] = packed_x[s]
            for a in range(2):
                syb[s, a, f] = packed_y[s][a]

    def copy_x(s, there):
        return pltpu.make_async_remote_copy(
            src_ref=sxb.at[s],
            dst_ref=rx.at[there],
            send_sem=x_send.at[s],
            recv_sem=x_recv.at[there],
            device_id=(to_x[s], py),
            device_id_type=MESH,
        )

    def copy_y(s, there):
        return pltpu.make_async_remote_copy(
            src_ref=syb.at[s],
            dst_ref=ry.at[there],
            send_sem=y_send.at[s],
            recv_sem=y_recv.at[there],
            device_id=(px, to_y[s]),
            device_id_type=MESH,
        )

    def copy_c(i, j, there):
        return pltpu.make_async_remote_copy(
            src_ref=syb.at[j, i],
            dst_ref=rc.at[there],
            send_sem=c_send.at[2 * i + j],
            recv_sem=c_recv.at[there],
            device_id=(to_x[i], to_y[j]),
            device_id_type=MESH,
        )

    for s in range(2):

        @pl.when(has_y[s])
        def _(s=s):
            copy_y(s, 1 - s).start()

    for i, j in corners:

        @pl.when(has_corner(i, j))
        def _(i=i, j=j):
            copy_c(i, j, 3 - 2 * i - j).start()

    for s in range(2):

        @pl.when(has_x[s])
        def _(s=s):
            copy_x(s, 1 - s).start()

    over(npx, lambda d: copy_g1(d).wait())
    column = g1[0]
    for d in range(1, npx):
        column += g1[d]
    g2[0] = column
    over(npy, lambda d: copy_g2(d).start())

    for s in range(2):

        @pl.when(has_x[s])
        def _(s=s):
            copy_x(s, s).wait()

    for s in range(2):

        @pl.when(has_y[s])
        def _(s=s):
            copy_y(s, s).wait()

    for i, j in corners:

        @pl.when(has_corner(i, j))
        def _(i=i, j=j):
            copy_c(i, j, 2 * i + j).wait()

    for f in range(FREQS):
        from_x = [rx[s, f] for s in range(2)]
        from_y = []
        for s in range(2):
            side = []
            for a in range(2):
                corner = lane_roll(rc[2 * a + s, f], 7 * (2 * a - 1))
                side.append(ry[s, a, f] + jnp.where(at_i[a], corner, 0.0))
            from_y.append(side)
        for m in range(CHANNELS):
            for a in range(2):
                block = held[f, 2 * m + a]
                block += jnp.where(at_i[a], lane_roll(from_x[a], 7 * a - m), 0.0)
                for s in range(2):
                    block += jnp.where(
                        at_j[s], lane_roll(from_y[s][a], 8 * (7 * s - m)), 0.0
                    )
                out_ref[pl.ds(128 * f + 64 * a + m, 8, stride=8), :] = block

    over(npy, lambda d: copy_g2(d).wait())
    if npy <= 8:
        column = g2[0]
        for d in range(1, npy):
            column += g2[d]
    else:
        column = lax.fori_loop(1, npy, lambda d, carry: carry + g2[d], g2[0])
    first_tile = TILE_DEV * (px * npy + py)
    pieces = [
        jnp.sum(jnp.where(wide == first_tile + q, column, 0.0), axis=1, keepdims=True)
        for q in range(TILE_DEV)
    ]
    grad_ref[...] = jnp.concatenate(pieces, axis=1)[:FREQS].T


def on_device(npx, npy, adjoint, zone_ids, resist, tile_map, materials):
    f32 = jnp.float32
    view = adjoint.reshape(2, 8, 8, 128).transpose(0, 2, 1, 3).reshape(128, 128)
    width = -(-TILE_DEV * npx * npy // 128) * 128
    vmem = pl.BlockSpec(memory_space=pltpu.VMEM)
    hbm = pl.BlockSpec(memory_space=pltpu.HBM)
    smem = pltpu.SMEM
    dma = pltpu.SemaphoreType.DMA
    out, grad = pl.pallas_call(
        functools.partial(body, npx, npy),
        out_shape=(
            jax.ShapeDtypeStruct((FREQS * 128, 128), f32),
            jax.ShapeDtypeStruct((TILE_DEV, FREQS), f32),
        ),
        in_specs=[hbm] * 8,
        out_specs=(vmem, vmem),
        scratch_shapes=[
            pltpu.VMEM((128, 128), f32),
            smem(zone_ids.shape, jnp.int32),
            smem(resist.shape, f32),
            smem(tile_map.shape, jnp.int32),
            smem(materials.shape, f32),
            pltpu.VMEM((1152, 128), jnp.bfloat16),
            pltpu.VMEM((1152, 128), jnp.bfloat16),
            pltpu.VMEM((16, 128), f32),
            dma((8,)),
            pltpu.VMEM((FREQS, 16, 8, 128), f32),
            pltpu.VMEM((2, FREQS, 8, 128), f32),
            pltpu.VMEM((2, 2, FREQS, 8, 128), f32),
            pltpu.VMEM((2, FREQS, 8, 128), f32),
            pltpu.VMEM((2, 2, FREQS, 8, 128), f32),
            pltpu.VMEM((4, FREQS, 8, 128), f32),
            pltpu.VMEM((npx, 8, width), f32),
            pltpu.VMEM((npy, 8, width), f32),
            dma((2,)),
            dma((2,)),
            dma((2,)),
            dma((2,)),
            dma((4,)),
            dma((4,)),
            dma((npx,)),
            dma((npx,)),
            dma((npy,)),
            dma((npy,)),
        ],
        compiler_params=pltpu.CompilerParams(
            collective_id=0, has_side_effects=True, vmem_limit_bytes=63 * 1024 * 1024
        ),
    )(view, zone_ids, resist, tile_map, materials, *[jnp.asarray(item) for item in tables()])
    applied = out.reshape(FREQS, 2, 8, 8, 128).transpose(0, 1, 3, 2, 4)
    return (applied.reshape(FREQS, 2, 1, CHANNELS, 1024), grad.T)


def solution(mesh):
    in_specs = (
        P("px", "py", None, None),
        P("px", "py", None),
        P("px", "py", None),
        P("px", "py", None),
        P(),
    )
    out_specs = (P(None, "px", "py", None, None), P(None, ("px", "py")))
    return jax.shard_map(
        functools.partial(on_device, mesh.shape["px"], mesh.shape["py"]),
        mesh=mesh,
        in_specs=in_specs,
        out_specs=out_specs,
        check_vma=False,
    )
```

```python
import functools

import jax
import jax.numpy as jnp
import ml_dtypes
import numpy as np
from jax import lax
from jax.experimental import pallas as pl
from jax.experimental.pallas import tpu as pltpu
from jax.sharding import PartitionSpec as P

NP = 8
FREQS = 3
TILE_DEV = 2
CHANNELS = 8
GRAD_SCALE = 0.001
MESH = pl.DeviceIdType.MESH


def legendre_values(points, point_count):
    values = np.zeros((points.shape[0], point_count))
    values[:, 0] = 1.0
    values[:, 1] = points
    for degree in range(2, point_count):
        values[:, degree] = (
            (2 * degree - 1) * points * values[:, degree - 1] - (degree - 1) * values[:, degree - 2]
        ) / degree
    return values


def lobatto(point_count):
    degree_top = point_count - 1
    points = np.cos(np.pi * np.arange(point_count) / degree_top)
    for newton_step in range(40):
        values = legendre_values(points, point_count)
        points = points - (points * values[:, degree_top] - values[:, degree_top - 1]) / (
            point_count * values[:, degree_top]
        )
    points = points[::-1]
    top_values = legendre_values(points, point_count)[:, degree_top]
    weights = 2.0 / (degree_top * point_count * top_values**2)
    differ = np.zeros((point_count, point_count))
    for row_index in range(point_count):
        for column_index in range(point_count):
            if row_index != column_index:
                differ[row_index, column_index] = top_values[row_index] / (
                    top_values[column_index] * (points[row_index] - points[column_index])
                )
    differ[0, 0] = -degree_top * point_count / 4.0
    differ[degree_top, degree_top] = degree_top * point_count / 4.0
    return (weights, differ)


def split_np(matrix):
    matrix = matrix.astype(np.float32)
    hi = matrix.astype(ml_dtypes.bfloat16)
    lo = (matrix - hi.astype(np.float32)).astype(ml_dtypes.bfloat16)
    return hi, lo


def tables():
    weights, differ = lobatto(NP)
    order = np.array([0, 2, 4, 6, 1, 3, 5, 7])
    weight = weights[order][:, None] * np.tile(np.kron(weights, weights), 2)[None, :]
    along_i = np.kron(np.eye(16), differ)
    along_j = np.kron(np.eye(2), np.kron(differ, np.eye(8)))
    along_k = np.kron(np.eye(16), differ[order][:, order])
    fwd_hi, fwd_lo = split_np(np.concatenate([along_i.T, along_j.T], axis=1))
    back_hi, back_lo = split_np(np.concatenate([along_i, along_j], axis=0))
    k_hi, k_lo = split_np(along_k)
    kt_hi, kt_lo = split_np(along_k.T)
    forward = np.concatenate([fwd_hi, fwd_lo, fwd_hi], axis=0)
    return (
        np.concatenate([forward[:, :128], forward[:, 128:], k_hi, k_hi, k_lo], axis=0),
        np.concatenate([back_hi, back_lo, back_hi, kt_hi, kt_hi, kt_lo], axis=0),
        np.tile(weight, (2, 1)).astype(np.float32),
    )


def split(values):
    hi = values.astype(jnp.bfloat16)
    lo = (values - hi.astype(jnp.float32)).astype(jnp.bfloat16)
    return hi, lo


def conj_times(c, x):
    return (c[0] * x[0] + c[1] * x[1], c[0] * x[1] - c[1] * x[0])


def plus(left, right):
    return (left[0] + right[0], left[1] + right[1])


def minus(left, right):
    return (left[0] - right[0], left[1] - right[1])


def body(
    npx,
    npy,
    x_hbm,
    zone_hbm,
    resist_hbm,
    tile_hbm,
    mat_hbm,
    forward_hbm,
    backward_hbm,
    weight_hbm,
    out_ref,
    grad_ref,
    x_ref,
    zone_ref,
    resist_ref,
    tile_ref,
    mat_ref,
    forward_ref,
    backward_ref,
    weight_ref,
    load_sem,
    held,
    sxb,
    syb,
    rx,
    ry,
    rc,
    shares,
    parts,
    x_send,
    x_recv,
    y_send,
    y_recv,
    c_send,
    c_recv,
    g_send,
    g_recv,
):
    f32 = jnp.float32
    loads = [
        pltpu.make_async_copy(source, target, load_sem.at[n])
        for n, (source, target) in enumerate(
            (
                (x_hbm, x_ref),
                (forward_hbm, forward_ref),
                (weight_hbm, weight_ref),
                (zone_hbm, zone_ref),
                (resist_hbm, resist_ref),
                (mat_hbm, mat_ref),
                (tile_hbm, tile_ref),
                (backward_hbm, backward_ref),
            )
        )
    ]
    for load in loads:
        load.start()
    px, py = lax.axis_index("px"), lax.axis_index("py")
    to_x = (px - 1, px + 1)
    to_y = (py - 1, py + 1)
    has_x = (px > 0, px < npx - 1)
    has_y = (py > 0, py < npy - 1)
    corners = [(i, j) for i in range(2) for j in range(2)]

    def has_corner(i, j):
        return jnp.logical_and(has_x[i], has_y[j])

    count = npx * npy
    me = px * npy + py

    def peer(d):
        other = lax.rem(me + d, count)
        return (other // npy, lax.rem(other, npy))

    def each_peer(step):
        if count <= 32:
            for d in range(1, count):
                step(d)
        else:
            lax.fori_loop(1, count, lambda d, carry: (step(d), carry)[1], 0)

    barrier = pltpu.get_barrier_semaphore()

    def greet(device):
        pl.semaphore_signal(barrier, inc=1, device_id=device, device_id_type=MESH)

    each_peer(lambda d: greet(peer(d)))

    row = lax.broadcasted_iota(jnp.int32, (8, 128), 0)
    lane = lax.broadcasted_iota(jnp.int32, (8, 128), 1)
    low = lane < 64
    keep = (row < 4) == low
    at_i = (lane % 8 == 0, lane % 8 == 7)
    at_j = ((lane // 8) % 8 == 0, (lane // 8) % 8 == 7)
    slot_i = [lane % 8 == m for m in range(8)]
    slot_j = [(lane // 8) % 8 == m for m in range(8)]
    seam_low = jnp.logical_and(row == 3, lane >= 64)
    seam_high = jnp.logical_and(row == 4, low)

    def lane_roll(block, shift):
        shift = shift % 128
        return block if shift == 0 else pltpu.roll(block, shift, 1)

    def swap(block):
        return jnp.where(keep, block, pltpu.roll(lane_roll(block, 64), 4, 0))

    for i in range(2):

        @pl.when(jnp.logical_not(has_x[i]))
        def _(i=i):
            rx[i] = jnp.zeros((FREQS, 8, 128), f32)

        @pl.when(jnp.logical_not(has_y[i]))
        def _(i=i):
            ry[i] = jnp.zeros((2, FREQS, 8, 128), f32)

    for i, j in corners:

        @pl.when(jnp.logical_not(has_corner(i, j)))
        def _(i=i, j=j):
            rc[2 * i + j] = jnp.zeros((FREQS, 8, 128), f32)

    loads[0].wait()
    blocks = []
    for m in range(CHANNELS):
        for a in range(2):
            blocks.append(swap(x_ref[pl.ds(64 * a + m, 8, stride=8), :]))
    nodal = jnp.concatenate(blocks, axis=0)
    hi, lo = split(nodal)
    loads[1].wait()
    wide_nodal = jnp.concatenate([hi, hi, lo], axis=1)
    first = jnp.dot(wide_nodal, forward_ref[0:384, :], preferred_element_type=f32)
    second = jnp.dot(wide_nodal, forward_ref[384:768, :], preferred_element_type=f32)

    def left(ref, base, tall):
        k_parts = [ref[base + 128 * n : base + 128 * n + 128, :] for n in range(3)]
        return jnp.dot(jnp.concatenate(k_parts, axis=1), tall, preferred_element_type=f32)

    third = left(forward_ref, 768, jnp.concatenate([hi, lo, hi], axis=0))
    raw = (first, second, third)
    loads[2].wait()
    weight = weight_ref[...]

    def channel(source, m):
        return source[16 * m : 16 * m + 16]

    def pair(source, m):
        return (weight * channel(source, m), weight * channel(source, m + 4))

    u = [pair(nodal, m) for m in range(4)]
    g = [[pair(raw[d], m) for m in range(4)] for d in range(3)]

    for load in loads[3:7]:
        load.wait()
    zones = [[zone_ref[a, 0, c] for c in range(2)] for a in range(2)]

    def spread(get):
        return jnp.concatenate(
            [jnp.where(low, get(a, 0), get(a, 1)) for a in range(2)], axis=0
        )

    resist = spread(lambda a, c: resist_ref[a, 0, c])
    coeffs = []
    slopes = []
    for f in range(FREQS):
        col = [spread(lambda a, c: mat_ref[f, zones[a][c], n]) for n in range(14)]
        density, gain = col[10], col[11]
        damping = resist * gain
        inverse = 1.0 / (density * density + damping * damping)
        real, imag = density * inverse, damping * inverse
        mobility = (col[8] * real - col[9] * imag, col[8] * imag + col[9] * real)
        square = gain * inverse * inverse
        real = -2.0 * density * damping * square
        imag = (density * density - damping * damping) * square
        slopes.append((col[8] * real - col[9] * imag, col[8] * imag + col[9] * real))
        coeffs.append(
            (
                (col[0], col[1]),
                (col[2], col[3]),
                (col[4], col[5]),
                (col[6], col[7]),
                mobility,
                (col[12], col[13]),
            )
        )

    energy_real = jnp.zeros((16, 128), f32)
    energy_imag = jnp.zeros((16, 128), f32)
    for d in range(3):
        real, imag = channel(raw[d], 3), channel(raw[d], 7)
        energy_real += g[d][3][0] * real - g[d][3][1] * imag
        energy_imag += g[d][3][0] * imag
    energy_imag = 2.0 * energy_imag
    owner = lax.broadcasted_iota(jnp.int32, (count, 128), 0)
    place = lax.broadcasted_iota(jnp.int32, (count, 128), 1)
    tile_at = jnp.where(place < TILE_DEV * FREQS, TILE_DEV * owner + place // FREQS, -1)
    freq_at = lax.broadcasted_iota(jnp.int32, (1, 128), 1) % FREQS
    densities = [
        GRAD_SCALE * (slopes[f][0] * energy_real + slopes[f][1] * energy_imag)
        for f in range(FREQS)
    ]
    table = jnp.zeros((count, 128), f32)
    for a in range(2):
        sums = [
            jnp.sum(item[8 * a : 8 * a + 8], axis=0, keepdims=True) for item in densities
        ]
        for c in range(2):
            entry = jnp.zeros((1, 128), f32)
            for f in range(FREQS):
                half = jnp.where(low[:1] == (c == 0), sums[f], 0.0)
                entry = jnp.where(freq_at == f, jnp.sum(half, axis=1, keepdims=True), entry)
            table += jnp.where(tile_at == tile_ref[a, 0, c], entry, 0.0)
    shares[...] = table

    pl.semaphore_wait(barrier, count - 1)

    def send_share(d):
        device = peer(d)
        pltpu.make_async_remote_copy(
            src_ref=shares.at[pl.ds(lax.rem(me + d, count), 1)],
            dst_ref=parts.at[pl.ds(d, 1)],
            send_sem=g_send.at[0],
            recv_sem=g_recv.at[0],
            device_id=device,
            device_id_type=MESH,
        ).start()

    each_peer(send_share)

    div = plus(plus(g[0][0], g[1][1]), g[2][2])
    sym = {}
    for m in range(3):
        for d in range(m, 3):
            sym[m, d] = plus(g[d][m], g[m][d])

    loads[7].wait()
    for f in range(FREQS):
        lame, shear, inertia, coupling, mobility, storage = coeffs[f]
        lame_term = conj_times(lame, div)
        stress = {}
        for (m, d), value in sym.items():
            item = conj_times(shear, value)
            if m == d:
                item = plus(item, lame_term)
            stress[m, d] = stress[d, m] = item
        flux = []
        for d in range(3):
            fluid = minus(conj_times(mobility, g[d][3]), conj_times(coupling, u[d]))
            items = [stress[m, d] for m in range(3)] + [fluid]
            flux.append(
                split(
                    jnp.concatenate([item[0] for item in items] + [item[1] for item in items], axis=0)
                )
            )
        items = [
            plus(conj_times(inertia, u[m]), conj_times(coupling, g[m][3])) for m in range(3)
        ] + [conj_times(storage, u[3])]
        local = jnp.concatenate([item[0] for item in items] + [item[1] for item in items], axis=0)
        (i_hi, i_lo), (j_hi, j_lo), (k_hi, k_lo) = flux
        total = jnp.dot(
            jnp.concatenate([i_hi, j_hi, i_hi, j_hi, i_lo, j_lo], axis=1),
            backward_ref[0:768, :],
            preferred_element_type=f32,
        )
        total += left(backward_ref, 768, jnp.concatenate([k_hi, k_lo, k_hi], axis=0))
        total -= local
        packed_x = [jnp.zeros((8, 128), f32)] * 2
        packed_y = [[jnp.zeros((8, 128), f32)] * 2 for _ in range(2)]
        for m in range(CHANNELS):
            both = []
            for a in range(2):
                block = swap(total[16 * m + 8 * a : 16 * m + 8 * a + 8])
                turned = lane_roll(block, 64)
                block = (
                    block
                    + jnp.where(seam_low, pltpu.roll(turned, 7, 0), 0.0)
                    + jnp.where(seam_high, pltpu.roll(turned, 1, 0), 0.0)
                )
                both.append(block)
            lower, upper = both
            both = [
                lower + jnp.where(at_i[1], lane_roll(upper, 7), 0.0),
                upper + jnp.where(at_i[0], lane_roll(lower, -7), 0.0),
            ]
            for s in range(2):
                packed_x[s] = jnp.where(slot_i[m], lane_roll(both[s], m - 7 * s), packed_x[s])
                for a in range(2):
                    packed_y[s][a] = jnp.where(
                        slot_j[m], lane_roll(both[a], 8 * (m - 7 * s)), packed_y[s][a]
                    )
            for a in range(2):
                held[f, 2 * m + a] = both[a]
        for s in range(2):
            sxb[s, f] = packed_x[s]
            for a in range(2):
                syb[s, a, f] = packed_y[s][a]

    def copy_x(s, there):
        return pltpu.make_async_remote_copy(
            src_ref=sxb.at[s],
            dst_ref=rx.at[there],
            send_sem=x_send.at[s],
            recv_sem=x_recv.at[there],
            device_id=(to_x[s], py),
            device_id_type=MESH,
        )

    def copy_y(s, there):
        return pltpu.make_async_remote_copy(
            src_ref=syb.at[s],
            dst_ref=ry.at[there],
            send_sem=y_send.at[s],
            recv_sem=y_recv.at[there],
            device_id=(px, to_y[s]),
            device_id_type=MESH,
        )

    def copy_c(i, j, there):
        return pltpu.make_async_remote_copy(
            src_ref=syb.at[j, i],
            dst_ref=rc.at[there],
            send_sem=c_send.at[2 * i + j],
            recv_sem=c_recv.at[there],
            device_id=(to_x[i], to_y[j]),
            device_id_type=MESH,
        )

    for s in range(2):

        @pl.when(has_y[s])
        def _(s=s):
            copy_y(s, 1 - s).start()

    for i, j in corners:

        @pl.when(has_corner(i, j))
        def _(i=i, j=j):
            copy_c(i, j, 3 - 2 * i - j).start()

    for s in range(2):

        @pl.when(has_x[s])
        def _(s=s):
            copy_x(s, 1 - s).start()

    for s in range(2):

        @pl.when(has_x[s])
        def _(s=s):
            copy_x(s, s).wait()

    for s in range(2):

        @pl.when(has_y[s])
        def _(s=s):
            copy_y(s, s).wait()

    for i, j in corners:

        @pl.when(has_corner(i, j))
        def _(i=i, j=j):
            copy_c(i, j, 2 * i + j).wait()

    for f in range(FREQS):
        from_x = [rx[s, f] for s in range(2)]
        from_y = []
        for s in range(2):
            side = []
            for a in range(2):
                corner = lane_roll(rc[2 * a + s, f], 7 * (2 * a - 1))
                side.append(ry[s, a, f] + jnp.where(at_i[a], corner, 0.0))
            from_y.append(side)
        for m in range(CHANNELS):
            for a in range(2):
                block = held[f, 2 * m + a]
                block += jnp.where(at_i[a], lane_roll(from_x[a], 7 * a - m), 0.0)
                for s in range(2):
                    block += jnp.where(
                        at_j[s], lane_roll(from_y[s][a], 8 * (7 * s - m)), 0.0
                    )
                out_ref[pl.ds(128 * f + 64 * a + m, 8, stride=8), :] = block

    others = pl.ds(1, count - 1)
    pltpu.make_async_copy(shares.at[others], parts.at[others], g_send.at[0]).wait()
    pltpu.make_async_copy(shares.at[others], parts.at[others], g_recv.at[0]).wait()
    parts[0:1] = shares[pl.ds(me, 1)]
    total = jnp.sum(parts[...], axis=0, keepdims=True)
    grad_ref[...] = jnp.concatenate(
        [total[:, FREQS * q : FREQS * q + FREQS] for q in range(TILE_DEV)], axis=0
    )


def on_device(npx, npy, adjoint, zone_ids, resist, tile_map, materials):
    f32 = jnp.float32
    view = adjoint.reshape(2, 8, 8, 128).transpose(0, 2, 1, 3).reshape(128, 128)
    vmem = pl.BlockSpec(memory_space=pltpu.VMEM)
    hbm = pl.BlockSpec(memory_space=pltpu.HBM)
    smem = pltpu.SMEM
    dma = pltpu.SemaphoreType.DMA
    out, grad = pl.pallas_call(
        functools.partial(body, npx, npy),
        out_shape=(
            jax.ShapeDtypeStruct((FREQS * 128, 128), f32),
            jax.ShapeDtypeStruct((TILE_DEV, FREQS), f32),
        ),
        in_specs=[hbm] * 8,
        out_specs=(vmem, vmem),
        scratch_shapes=[
            pltpu.VMEM((128, 128), f32),
            smem(zone_ids.shape, jnp.int32),
            smem(resist.shape, f32),
            smem(tile_map.shape, jnp.int32),
            smem(materials.shape, f32),
            pltpu.VMEM((1152, 128), jnp.bfloat16),
            pltpu.VMEM((1152, 128), jnp.bfloat16),
            pltpu.VMEM((16, 128), f32),
            dma((8,)),
            pltpu.VMEM((FREQS, 16, 8, 128), f32),
            pltpu.VMEM((2, FREQS, 8, 128), f32),
            pltpu.VMEM((2, 2, FREQS, 8, 128), f32),
            pltpu.VMEM((2, FREQS, 8, 128), f32),
            pltpu.VMEM((2, 2, FREQS, 8, 128), f32),
            pltpu.VMEM((4, FREQS, 8, 128), f32),
            pltpu.VMEM((npx * npy, 128), f32),
            pltpu.VMEM((npx * npy, 128), f32),
            dma((2,)),
            dma((2,)),
            dma((2,)),
            dma((2,)),
            dma((4,)),
            dma((4,)),
            dma((1,)),
            dma((1,)),
        ],
        compiler_params=pltpu.CompilerParams(
            collective_id=0, has_side_effects=True, vmem_limit_bytes=63 * 1024 * 1024
        ),
    )(view, zone_ids, resist, tile_map, materials, *[jnp.asarray(item) for item in tables()])
    applied = out.reshape(FREQS, 2, 8, 8, 128).transpose(0, 1, 3, 2, 4)
    return (applied.reshape(FREQS, 2, 1, CHANNELS, 1024), grad.T)


def solution(mesh):
    in_specs = (
        P("px", "py", None, None),
        P("px", "py", None),
        P("px", "py", None),
        P("px", "py", None),
        P(),
    )
    out_specs = (P(None, "px", "py", None, None), P(None, ("px", "py")))
    return jax.shard_map(
        functools.partial(on_device, mesh.shape["px"], mesh.shape["py"]),
        mesh=mesh,
        in_specs=in_specs,
        out_specs=out_specs,
        check_vma=False,
    )
```

```python
import functools

import jax
import jax.numpy as jnp
import ml_dtypes
import numpy as np
from jax import lax
from jax.experimental import pallas as pl
from jax.experimental.pallas import tpu as pltpu
from jax.sharding import PartitionSpec as P

NP = 8
FREQS = 3
TILE_DEV = 2
CHANNELS = 8
GRAD_SCALE = 0.001
MESH = pl.DeviceIdType.MESH


def legendre_values(points, point_count):
    values = np.zeros((points.shape[0], point_count))
    values[:, 0] = 1.0
    values[:, 1] = points
    for degree in range(2, point_count):
        values[:, degree] = (
            (2 * degree - 1) * points * values[:, degree - 1] - (degree - 1) * values[:, degree - 2]
        ) / degree
    return values


def lobatto(point_count):
    degree_top = point_count - 1
    points = np.cos(np.pi * np.arange(point_count) / degree_top)
    for newton_step in range(40):
        values = legendre_values(points, point_count)
        points = points - (points * values[:, degree_top] - values[:, degree_top - 1]) / (
            point_count * values[:, degree_top]
        )
    points = points[::-1]
    top_values = legendre_values(points, point_count)[:, degree_top]
    weights = 2.0 / (degree_top * point_count * top_values**2)
    differ = np.zeros((point_count, point_count))
    for row_index in range(point_count):
        for column_index in range(point_count):
            if row_index != column_index:
                differ[row_index, column_index] = top_values[row_index] / (
                    top_values[column_index] * (points[row_index] - points[column_index])
                )
    differ[0, 0] = -degree_top * point_count / 4.0
    differ[degree_top, degree_top] = degree_top * point_count / 4.0
    return (weights, differ)


def split_np(matrix):
    matrix = matrix.astype(np.float32)
    hi = matrix.astype(ml_dtypes.bfloat16)
    lo = (matrix - hi.astype(np.float32)).astype(ml_dtypes.bfloat16)
    return hi, lo


def tables():
    weights, differ = lobatto(NP)
    order = np.array([0, 2, 4, 6, 1, 3, 5, 7])
    weight = weights[order][:, None] * np.tile(np.kron(weights, weights), 2)[None, :]
    along_i = np.kron(np.eye(16), differ)
    along_j = np.kron(np.eye(2), np.kron(differ, np.eye(8)))
    along_k = np.kron(np.eye(16), differ[order][:, order])
    fwd_hi, fwd_lo = split_np(np.concatenate([along_i.T, along_j.T], axis=1))
    back_hi, back_lo = split_np(np.concatenate([along_i, along_j], axis=0))
    k_hi, k_lo = split_np(along_k)
    kt_hi, kt_lo = split_np(along_k.T)
    forward = np.concatenate([fwd_hi, fwd_lo, fwd_hi], axis=0)
    return (
        np.concatenate([forward[:, :128], forward[:, 128:], k_hi, k_hi, k_lo], axis=0),
        np.concatenate([back_hi, back_lo, back_hi, kt_hi, kt_hi, kt_lo], axis=0),
        np.tile(weight, (2, 1)).astype(np.float32),
    )


def split(values):
    hi = values.astype(jnp.bfloat16)
    lo = (values - hi.astype(jnp.float32)).astype(jnp.bfloat16)
    return hi, lo


def conj_times(c, x):
    return (c[0] * x[0] + c[1] * x[1], c[0] * x[1] - c[1] * x[0])


def plus(left, right):
    return (left[0] + right[0], left[1] + right[1])


def minus(left, right):
    return (left[0] - right[0], left[1] - right[1])


def body(
    npx,
    npy,
    x_hbm,
    zone_hbm,
    resist_hbm,
    tile_hbm,
    mat_hbm,
    forward_hbm,
    backward_hbm,
    weight_hbm,
    out_hbm,
    grad_ref,
    x_ref,
    zone_ref,
    resist_ref,
    tile_ref,
    mat_ref,
    forward_ref,
    backward_ref,
    weight_ref,
    load_sem,
    out_ref,
    store_sem,
    held,
    sxb,
    syb,
    rx,
    ry,
    rc,
    shares,
    parts,
    x_send,
    x_recv,
    y_send,
    y_recv,
    c_send,
    c_recv,
    g_send,
    g_recv,
):
    f32 = jnp.float32
    loads = [
        pltpu.make_async_copy(source, target, load_sem.at[n])
        for n, (source, target) in enumerate(
            (
                (x_hbm, x_ref),
                (forward_hbm, forward_ref),
                (weight_hbm, weight_ref),
                (zone_hbm, zone_ref),
                (resist_hbm, resist_ref),
                (mat_hbm, mat_ref),
                (tile_hbm, tile_ref),
                (backward_hbm, backward_ref),
            )
        )
    ]
    for load in loads:
        load.start()
    px, py = lax.axis_index("px"), lax.axis_index("py")
    to_x = (px - 1, px + 1)
    to_y = (py - 1, py + 1)
    has_x = (px > 0, px < npx - 1)
    has_y = (py > 0, py < npy - 1)
    corners = [(i, j) for i in range(2) for j in range(2)]

    def has_corner(i, j):
        return jnp.logical_and(has_x[i], has_y[j])

    count = npx * npy
    me = px * npy + py

    def peer(d):
        other = lax.rem(me + d, count)
        return (other // npy, lax.rem(other, npy))

    def each_peer(step):
        if count <= 32:
            for d in range(1, count):
                step(d)
        else:
            lax.fori_loop(1, count, lambda d, carry: (step(d), carry)[1], 0)

    barrier = pltpu.get_barrier_semaphore()

    def greet(device):
        pl.semaphore_signal(barrier, inc=1, device_id=device, device_id_type=MESH)

    each_peer(lambda d: greet(peer(d)))

    row = lax.broadcasted_iota(jnp.int32, (8, 128), 0)
    lane = lax.broadcasted_iota(jnp.int32, (8, 128), 1)
    low = lane < 64
    keep = (row < 4) == low
    at_i = (lane % 8 == 0, lane % 8 == 7)
    at_j = ((lane // 8) % 8 == 0, (lane // 8) % 8 == 7)
    slot_i = [lane % 8 == m for m in range(8)]
    slot_j = [(lane // 8) % 8 == m for m in range(8)]
    seam_low = jnp.logical_and(row == 3, lane >= 64)
    seam_high = jnp.logical_and(row == 4, low)

    def lane_roll(block, shift):
        shift = shift % 128
        return block if shift == 0 else pltpu.roll(block, shift, 1)

    def swap(block):
        return jnp.where(keep, block, pltpu.roll(lane_roll(block, 64), 4, 0))

    for i in range(2):

        @pl.when(jnp.logical_not(has_x[i]))
        def _(i=i):
            rx[i] = jnp.zeros((FREQS, 8, 128), f32)

        @pl.when(jnp.logical_not(has_y[i]))
        def _(i=i):
            ry[i] = jnp.zeros((2, FREQS, 8, 128), f32)

    for i, j in corners:

        @pl.when(jnp.logical_not(has_corner(i, j)))
        def _(i=i, j=j):
            rc[2 * i + j] = jnp.zeros((FREQS, 8, 128), f32)

    loads[0].wait()
    blocks = []
    for m in range(CHANNELS):
        for a in range(2):
            blocks.append(swap(x_ref[pl.ds(64 * a + m, 8, stride=8), :]))
    nodal = jnp.concatenate(blocks, axis=0)
    hi, lo = split(nodal)
    loads[1].wait()
    wide_nodal = jnp.concatenate([hi, hi, lo], axis=1)
    first = jnp.dot(wide_nodal, forward_ref[0:384, :], preferred_element_type=f32)
    second = jnp.dot(wide_nodal, forward_ref[384:768, :], preferred_element_type=f32)

    def left(ref, base, tall):
        k_parts = [ref[base + 128 * n : base + 128 * n + 128, :] for n in range(3)]
        return jnp.dot(jnp.concatenate(k_parts, axis=1), tall, preferred_element_type=f32)

    third = left(forward_ref, 768, jnp.concatenate([hi, lo, hi], axis=0))
    raw = (first, second, third)
    loads[2].wait()
    weight = weight_ref[...]

    def channel(source, m):
        return source[16 * m : 16 * m + 16]

    def pair(source, m):
        return (weight * channel(source, m), weight * channel(source, m + 4))

    u = [pair(nodal, m) for m in range(4)]
    g = [[pair(raw[d], m) for m in range(4)] for d in range(3)]

    for load in loads[3:7]:
        load.wait()
    zones = [[zone_ref[a, 0, c] for c in range(2)] for a in range(2)]

    def spread(get):
        return jnp.concatenate(
            [jnp.where(low, get(a, 0), get(a, 1)) for a in range(2)], axis=0
        )

    resist = spread(lambda a, c: resist_ref[a, 0, c])
    coeffs = []
    slopes = []
    for f in range(FREQS):
        col = [spread(lambda a, c: mat_ref[f, zones[a][c], n]) for n in range(14)]
        density, gain = col[10], col[11]
        damping = resist * gain
        inverse = 1.0 / (density * density + damping * damping)
        real, imag = density * inverse, damping * inverse
        mobility = (col[8] * real - col[9] * imag, col[8] * imag + col[9] * real)
        square = gain * inverse * inverse
        real = -2.0 * density * damping * square
        imag = (density * density - damping * damping) * square
        slopes.append((col[8] * real - col[9] * imag, col[8] * imag + col[9] * real))
        coeffs.append(
            (
                (col[0], col[1]),
                (col[2], col[3]),
                (col[4], col[5]),
                (col[6], col[7]),
                mobility,
                (col[12], col[13]),
            )
        )

    energy_real = jnp.zeros((16, 128), f32)
    energy_imag = jnp.zeros((16, 128), f32)
    for d in range(3):
        real, imag = channel(raw[d], 3), channel(raw[d], 7)
        energy_real += g[d][3][0] * real - g[d][3][1] * imag
        energy_imag += g[d][3][0] * imag
    energy_imag = 2.0 * energy_imag
    owner = lax.broadcasted_iota(jnp.int32, (count, 128), 0)
    place = lax.broadcasted_iota(jnp.int32, (count, 128), 1)
    tile_at = jnp.where(place < TILE_DEV * FREQS, TILE_DEV * owner + place // FREQS, -1)
    freq_at = lax.broadcasted_iota(jnp.int32, (1, 128), 1) % FREQS
    densities = [
        GRAD_SCALE * (slopes[f][0] * energy_real + slopes[f][1] * energy_imag)
        for f in range(FREQS)
    ]
    table = jnp.zeros((count, 128), f32)
    for a in range(2):
        sums = [
            jnp.sum(item[8 * a : 8 * a + 8], axis=0, keepdims=True) for item in densities
        ]
        for c in range(2):
            entry = jnp.zeros((1, 128), f32)
            for f in range(FREQS):
                half = jnp.where(low[:1] == (c == 0), sums[f], 0.0)
                entry = jnp.where(freq_at == f, jnp.sum(half, axis=1, keepdims=True), entry)
            table += jnp.where(tile_at == tile_ref[a, 0, c], entry, 0.0)
    shares[...] = table

    div = plus(plus(g[0][0], g[1][1]), g[2][2])
    sym = {}
    for m in range(3):
        for d in range(m, 3):
            sym[m, d] = plus(g[d][m], g[m][d])

    loads[7].wait()
    for f in range(FREQS):
        lame, shear, inertia, coupling, mobility, storage = coeffs[f]
        lame_term = conj_times(lame, div)
        stress = {}
        for (m, d), value in sym.items():
            item = conj_times(shear, value)
            if m == d:
                item = plus(item, lame_term)
            stress[m, d] = stress[d, m] = item
        flux = []
        for d in range(3):
            fluid = minus(conj_times(mobility, g[d][3]), conj_times(coupling, u[d]))
            items = [stress[m, d] for m in range(3)] + [fluid]
            flux.append(
                split(
                    jnp.concatenate([item[0] for item in items] + [item[1] for item in items], axis=0)
                )
            )
        items = [
            plus(conj_times(inertia, u[m]), conj_times(coupling, g[m][3])) for m in range(3)
        ] + [conj_times(storage, u[3])]
        local = jnp.concatenate([item[0] for item in items] + [item[1] for item in items], axis=0)
        (i_hi, i_lo), (j_hi, j_lo), (k_hi, k_lo) = flux
        total = jnp.dot(
            jnp.concatenate([i_hi, j_hi, i_hi, j_hi, i_lo, j_lo], axis=1),
            backward_ref[0:768, :],
            preferred_element_type=f32,
        )
        total += left(backward_ref, 768, jnp.concatenate([k_hi, k_lo, k_hi], axis=0))
        total -= local
        packed_x = [jnp.zeros((8, 128), f32)] * 2
        packed_y = [[jnp.zeros((8, 128), f32)] * 2 for _ in range(2)]
        for m in range(CHANNELS):
            both = []
            for a in range(2):
                block = swap(total[16 * m + 8 * a : 16 * m + 8 * a + 8])
                turned = lane_roll(block, 64)
                block = (
                    block
                    + jnp.where(seam_low, pltpu.roll(turned, 7, 0), 0.0)
                    + jnp.where(seam_high, pltpu.roll(turned, 1, 0), 0.0)
                )
                both.append(block)
            lower, upper = both
            both = [
                lower + jnp.where(at_i[1], lane_roll(upper, 7), 0.0),
                upper + jnp.where(at_i[0], lane_roll(lower, -7), 0.0),
            ]
            for s in range(2):
                packed_x[s] = jnp.where(slot_i[m], lane_roll(both[s], m - 7 * s), packed_x[s])
                for a in range(2):
                    packed_y[s][a] = jnp.where(
                        slot_j[m], lane_roll(both[a], 8 * (m - 7 * s)), packed_y[s][a]
                    )
            for a in range(2):
                held[f, 2 * m + a] = both[a]
        for s in range(2):
            sxb[s, f] = packed_x[s]
            for a in range(2):
                syb[s, a, f] = packed_y[s][a]

    pl.semaphore_wait(barrier, count - 1)

    def send_share(d):
        device = peer(d)
        pltpu.make_async_remote_copy(
            src_ref=shares.at[pl.ds(lax.rem(me + d, count), 1)],
            dst_ref=parts.at[pl.ds(d, 1)],
            send_sem=g_send.at[0],
            recv_sem=g_recv.at[0],
            device_id=device,
            device_id_type=MESH,
        ).start()

    each_peer(send_share)

    def copy_x(s, there):
        return pltpu.make_async_remote_copy(
            src_ref=sxb.at[s],
            dst_ref=rx.at[there],
            send_sem=x_send.at[s],
            recv_sem=x_recv.at[there],
            device_id=(to_x[s], py),
            device_id_type=MESH,
        )

    def copy_y(s, there):
        return pltpu.make_async_remote_copy(
            src_ref=syb.at[s],
            dst_ref=ry.at[there],
            send_sem=y_send.at[s],
            recv_sem=y_recv.at[there],
            device_id=(px, to_y[s]),
            device_id_type=MESH,
        )

    def copy_c(i, j, there):
        return pltpu.make_async_remote_copy(
            src_ref=syb.at[j, i],
            dst_ref=rc.at[there],
            send_sem=c_send.at[2 * i + j],
            recv_sem=c_recv.at[there],
            device_id=(to_x[i], to_y[j]),
            device_id_type=MESH,
        )

    for s in range(2):

        @pl.when(has_y[s])
        def _(s=s):
            copy_y(s, 1 - s).start()

    for i, j in corners:

        @pl.when(has_corner(i, j))
        def _(i=i, j=j):
            copy_c(i, j, 3 - 2 * i - j).start()

    for s in range(2):

        @pl.when(has_x[s])
        def _(s=s):
            copy_x(s, 1 - s).start()

    for s in range(2):

        @pl.when(has_x[s])
        def _(s=s):
            copy_x(s, s).wait()

    for s in range(2):

        @pl.when(has_y[s])
        def _(s=s):
            copy_y(s, s).wait()

    for i, j in corners:

        @pl.when(has_corner(i, j))
        def _(i=i, j=j):
            copy_c(i, j, 2 * i + j).wait()

    stores = []
    for f in range(FREQS):
        from_x = [rx[s, f] for s in range(2)]
        from_y = []
        for s in range(2):
            side = []
            for a in range(2):
                corner = lane_roll(rc[2 * a + s, f], 7 * (2 * a - 1))
                side.append(ry[s, a, f] + jnp.where(at_i[a], corner, 0.0))
            from_y.append(side)
        for m in range(CHANNELS):
            for a in range(2):
                block = held[f, 2 * m + a]
                block += jnp.where(at_i[a], lane_roll(from_x[a], 7 * a - m), 0.0)
                for s in range(2):
                    block += jnp.where(
                        at_j[s], lane_roll(from_y[s][a], 8 * (7 * s - m)), 0.0
                    )
                out_ref[pl.ds(128 * f + 64 * a + m, 8, stride=8), :] = block
        stores.append(
            pltpu.make_async_copy(
                out_ref.at[pl.ds(128 * f, 128)], out_hbm.at[pl.ds(128 * f, 128)], store_sem.at[f]
            )
        )
        stores[f].start()

    others = pl.ds(1, count - 1)
    pltpu.make_async_copy(shares.at[others], parts.at[others], g_send.at[0]).wait()
    pltpu.make_async_copy(shares.at[others], parts.at[others], g_recv.at[0]).wait()
    parts[0:1] = shares[pl.ds(me, 1)]
    total = jnp.sum(parts[...], axis=0, keepdims=True)
    grad_ref[...] = jnp.concatenate(
        [total[:, FREQS * q : FREQS * q + FREQS] for q in range(TILE_DEV)], axis=0
    )
    for store in stores:
        store.wait()


def hand_on(out_from, grad_from, out_to, grad_to, out_held, grad_held, in_sem, out_sem):
    chunks = in_sem.shape[0] - 1
    rows = out_from.shape[0] // chunks
    spans = [pl.ds(n * rows, rows) for n in range(chunks)]
    routes = [(grad_from, grad_held, grad_to)] + [
        (out_from.at[span], out_held.at[span], out_to.at[span]) for span in spans
    ]
    fetches = [
        pltpu.make_async_copy(route[0], route[1], in_sem.at[n]) for n, route in enumerate(routes)
    ]
    stores = [
        pltpu.make_async_copy(route[1], route[2], out_sem.at[n]) for n, route in enumerate(routes)
    ]
    for fetch in fetches:
        fetch.start()
    for fetch, store in zip(fetches, stores):
        fetch.wait()
        store.start()
    for store in stores:
        store.wait()


def on_device(npx, npy, adjoint, zone_ids, resist, tile_map, materials):
    f32 = jnp.float32
    view = adjoint.reshape(2, 8, 8, 128).transpose(0, 2, 1, 3).reshape(128, 128)
    vmem = pl.BlockSpec(memory_space=pltpu.VMEM)
    hbm = pl.BlockSpec(memory_space=pltpu.HBM)
    smem = pltpu.SMEM
    dma = pltpu.SemaphoreType.DMA
    out, grad = pl.pallas_call(
        functools.partial(body, npx, npy),
        out_shape=(
            jax.ShapeDtypeStruct((FREQS * 128, 128), f32),
            jax.ShapeDtypeStruct((TILE_DEV, FREQS), f32),
        ),
        in_specs=[hbm] * 8,
        out_specs=(hbm, vmem),
        scratch_shapes=[
            pltpu.VMEM((128, 128), f32),
            smem(zone_ids.shape, jnp.int32),
            smem(resist.shape, f32),
            smem(tile_map.shape, jnp.int32),
            smem(materials.shape, f32),
            pltpu.VMEM((1152, 128), jnp.bfloat16),
            pltpu.VMEM((1152, 128), jnp.bfloat16),
            pltpu.VMEM((16, 128), f32),
            dma((8,)),
            pltpu.VMEM((FREQS * 128, 128), f32),
            dma((FREQS,)),
            pltpu.VMEM((FREQS, 16, 8, 128), f32),
            pltpu.VMEM((2, FREQS, 8, 128), f32),
            pltpu.VMEM((2, 2, FREQS, 8, 128), f32),
            pltpu.VMEM((2, FREQS, 8, 128), f32),
            pltpu.VMEM((2, 2, FREQS, 8, 128), f32),
            pltpu.VMEM((4, FREQS, 8, 128), f32),
            pltpu.VMEM((npx * npy, 128), f32),
            pltpu.VMEM((npx * npy, 128), f32),
            dma((2,)),
            dma((2,)),
            dma((2,)),
            dma((2,)),
            dma((4,)),
            dma((4,)),
            dma((1,)),
            dma((1,)),
        ],
        compiler_params=pltpu.CompilerParams(
            collective_id=0, has_side_effects=True, vmem_limit_bytes=63 * 1024 * 1024
        ),
    )(view, zone_ids, resist, tile_map, materials, *[jnp.asarray(item) for item in tables()])
    chunks = 3
    out, grad = pl.pallas_call(
        hand_on,
        out_shape=(
            jax.ShapeDtypeStruct(out.shape, f32),
            jax.ShapeDtypeStruct(grad.shape, f32),
        ),
        in_specs=[hbm] * 2,
        out_specs=(hbm, hbm),
        scratch_shapes=[
            pltpu.VMEM(out.shape, f32),
            pltpu.VMEM(grad.shape, f32),
            dma((chunks + 1,)),
            dma((chunks + 1,)),
        ],
        compiler_params=pltpu.CompilerParams(vmem_limit_bytes=63 * 1024 * 1024),
    )(out, grad)
    applied = out.reshape(FREQS, 2, 8, 8, 128).transpose(0, 1, 3, 2, 4)
    return (applied.reshape(FREQS, 2, 1, CHANNELS, 1024), grad.T)


def solution(mesh):
    in_specs = (
        P("px", "py", None, None),
        P("px", "py", None),
        P("px", "py", None),
        P("px", "py", None),
        P(),
    )
    out_specs = (P(None, "px", "py", None, None), P(None, ("px", "py")))
    return jax.shard_map(
        functools.partial(on_device, mesh.shape["px"], mesh.shape["py"]),
        mesh=mesh,
        in_specs=in_specs,
        out_specs=out_specs,
        check_vma=False,
    )
```
